128 devices in a mesh: blk: 16 (over x, z_lo, core), rows: 8 (over y, z_hi).
Axes of the slice: x: 4, y: 4, z: 4 (z_hi: 2, z_lo: 2; z = z_hi * 2 + z_lo), core: 2. Of those that a mesh axis runs over, the one named last changes fastest.
Arguments:
- points: float32 [196608, 256], P(('blk', 'rows')), may hold values from -6 to 6
- centres: float32 [8192, 256], P('blk'), may hold values from -6 to 6
- coefficients: float32 [8192], P('blk'), may hold values from -0.0625 to 0.0625
Outputs:
- normal_product: float32 [8192], P('blk')
The draws below stay inside these ranges and needn't reach their ends.
All inputs are finite; a program needn't handle non-finite values.
Results may differ from the reference program's by a relative error of at most 0.0003.
Values sent between devices are 32-bit elements; how exact they have to be, the bound alone decides.
No kernel may reach another device: no remote copies, remote signals or barrier semaphores. Data moves between devices by JAX's collectives and lax.ppermute only.
A program may use at most 128 MiB of HBM per device.

```python
import math
import jax
import jax.numpy as jnp
from jax import lax

D = 256
C_DEV = 512
NPTS = 196608
M = 8192
N_BLK = 16


def draw_points(key, part):
    key = jax.random.fold_in(key, 11)
    return jnp.clip(jax.random.normal(key, (NPTS, D), jnp.float32), -6.0, 6.0)


def draw_centres(key, part):
    key = jax.random.fold_in(key, 23)
    return jnp.clip(jax.random.normal(key, (M, D), jnp.float32), -6.0, 6.0)


def block_scale(key, extent, cuts, smallest, high):
    gain = 1.0
    for dim, blocks in cuts:
        heights = jax.random.uniform(jax.random.fold_in(jax.random.fold_in(key, 6), dim), (blocks,), jnp.float32, smallest / len(cuts), high / len(cuts))
        gain = gain * jnp.repeat(jnp.exp(heights), extent[dim] // blocks).reshape((-1,) + (1,) * (len(extent) - 1 - dim))
    return gain


def bell_draw(rng, shape, deviation, most, split=(), dtype=jnp.bfloat16):
    factor_of = block_scale(rng, shape, split, -0.22, 0.18) if split else 1.0
    array = jax.random.normal(rng, shape, jnp.float32) * deviation * factor_of
    return jnp.minimum(jnp.maximum(array, -most), most).astype(dtype)


def setup_inputs(seed: int = 0) -> dict:
    arg_keys = jax.random.split(jax.random.key(seed), 4)
    points = draw_points(jax.random.fold_in(arg_keys[3], 71), 0)
    centres = draw_centres(jax.random.fold_in(arg_keys[3], 71), 0)
    coefficients = bell_draw(arg_keys[2], (M,), M ** -0.5, 0.0625, ((0, 16),), jnp.float32)
    return {"points": points, "centres": centres, "coefficients": coefficients}


def kernel_block(points, point_sq, block):
    width = points.shape[1]
    inner = jnp.dot(points, block.T, precision=lax.Precision.HIGHEST, preferred_element_type=jnp.float32)
    block_sq = lax.optimization_barrier(jnp.sum(block * block, axis=1))
    dist_sq = point_sq[:, None] + block_sq[None, :] - 2.0 * inner
    return jnp.exp((2.0 * width - dist_sq) * (0.5 / math.sqrt(width)))

def reference(points, centres, coefficients):
    point_sq = lax.optimization_barrier(jnp.sum(points * points, axis=1))
    blocks = centres.reshape(N_BLK, C_DEV, D)
    coef_blocks = coefficients.reshape(N_BLK, C_DEV)

    def add_block(carry, pair):
        block, coef = pair
        kernel = kernel_block(points, point_sq, block)
        return (carry + jnp.dot(kernel, coef, precision=lax.Precision.HIGHEST, preferred_element_type=jnp.float32), None)
    start = jnp.zeros((points.shape[0],), jnp.float32)
    point_values, unused = lax.scan(add_block, start, (blocks, coef_blocks))

    def project(block):
        kernel = kernel_block(points, point_sq, block)
        return jnp.dot(point_values, kernel, precision=lax.Precision.HIGHEST, preferred_element_type=jnp.float32)
    total = lax.map(project, blocks).reshape(M)
    return total / NPTS
```

```python
import functools
import math

import jax
import jax.numpy as jnp
from jax import lax
from jax.experimental import pallas as pl
from jax.experimental.pallas import tpu as pltpu
from jax.sharding import PartitionSpec as P

F32, BF16, F8 = jnp.float32, jnp.bfloat16, jnp.float8_e4m3fn
LOG2E = 1.4426950408889634
UNIT = 256
PACKED = 264
LIFT = 256.0
ROWS = 256
VMEM = pl.BlockSpec(memory_space=pltpu.VMEM)
HBM = pl.BlockSpec(memory_space=pltpu.HBM)


def constants(width):
    scale = LOG2E / math.sqrt(width)
    return scale, 0.5 * LOG2E * math.sqrt(width)


def prepare_points(x_ref, xh_ref, x8_ref, a_ref):
    scale, offset = constants(x_ref.shape[1])
    for q in range(0, x_ref.shape[0], ROWS):
        r = slice(q, q + ROWS)
        x = x_ref[r, :]
        high = x.astype(BF16)
        low = (x - high.astype(F32)) * LIFT
        xh_ref[r, :] = high
        x8_ref[r, :] = jnp.concatenate([x.astype(F8), low.astype(F8)], axis=1)
        a = jnp.sum(x * x, axis=1, keepdims=True) * (-0.5 * scale) + offset
        a_ref[r, :] = jnp.broadcast_to(a, (ROWS, 128))


def prepare_units(refs, wh_ref, w8_ref, b_ref, c_ref):
    i = 0
    for ref in refs:
        for j in range(ref.shape[0]):
            width = ref.shape[2]
            scale, offset = constants(width)
            t = ref[j, 0:UNIT, :].T
            scaled = t * scale
            high = scaled.astype(BF16)
            low = (scaled - high.astype(F32)) * (LIFT / scale)
            wh_ref[i] = high
            w8_ref[i] = jnp.concatenate([low.astype(F8), t.astype(F8)], axis=0)
            b_ref[i] = jnp.sum(t * t, axis=0, keepdims=True) * (-0.5 * scale) + offset
            c_ref[i] = ref[j, UNIT : UNIT + 1, :]
            i += 1


def tile(i, r, xh_ref, x8_ref, a_ref, wh_ref, w8_ref, b_ref, c_ref, k_ref):
    scale, _ = constants(xh_ref.shape[1])
    main = jnp.dot(xh_ref[r, :], wh_ref[i], preferred_element_type=F32)
    cross = jnp.dot(x8_ref[r, :], w8_ref[i], preferred_element_type=F32)
    a = a_ref[r, :]
    value = None
    for t in range(0, UNIT, 128):
        c = slice(t, t + 128)
        k = jnp.exp2(main[:, c] + cross[:, c] * (scale / LIFT) + a + b_ref[i, :, c])
        k_ref[i, r, c] = k
        term = k * c_ref[i, :, c]
        value = term if value is None else value + term
    return value


def first_product(group, points, prepared, v_in, v_ref, k_ref, saved=None, sem=None):
    units = k_ref.shape[0]
    assert units % group == 0
    rows = points[0].shape[0]

    def save(j, q):
        part = (pl.ds(j * group, group), pl.ds(q, ROWS))
        return pltpu.make_async_copy(k_ref.at[part], saved.at[part], sem)

    @pl.loop(0, units // group)
    def _(j):
        for q in range(0, rows, ROWS):
            r = slice(q, q + ROWS)
            value = None
            for u in range(group):
                term = tile(j * group + u, r, *points, *prepared, k_ref)
                value = term if value is None else value + term
            if v_in is None:
                before = jnp.where(j == 0, 0.0, v_ref[r, :])
            else:
                before = jnp.where(j == 0, v_in[r, :], v_ref[r, :])
            v_ref[r, :] = before + value
            if saved is not None:
                save(j, q).start()

    if saved is not None:
        pltpu.make_async_copy(k_ref, saved, sem).wait()


def opening_kernel(x_ref, *rest):
    units, (xh, x8, a, v, saved), (k, *prepared), sem = rest[:2], rest[2:7], rest[7:12], rest[12]
    prepare_points(x_ref, xh, x8, a)
    prepare_units(units, *prepared)
    v[...] = jnp.zeros_like(v)
    first_product(2, (xh, x8, a), prepared, None, v, k, saved, sem)


def middle_kernel(n, group, xh, x8, a, v_in, *rest):
    units, (v, saved), (k, *prepared), sem = rest[:n], rest[n : n + 2], rest[n + 2 : n + 7], rest[n + 7]
    prepare_units(units, *prepared)
    v[...] = v_in[...]
    first_product(group, (xh, x8, a), prepared, v_in, v, k, saved, sem)


def closing_kernel(n, m, group, place_ref, xh, x8, a, v_in, *rest):
    units, saved, out = rest[:n], rest[n : n + m], rest[n + m]
    v, sums, k, *more = rest[n + m + 1 :]
    prepared, held, sem = more[:4], more[4 : 4 + m], more[4 + m]
    copies = [pltpu.make_async_copy(saved[i], held[i], sem.at[i]) for i in range(m)]
    for copy in copies:
        copy.start()
    prepare_units(units, *prepared)
    first_product(group, (xh, x8, a), prepared, v_in, v, k)
    for q in range(0, v.shape[0], ROWS):
        r = slice(q, q + ROWS)
        v[r, :] = jnp.broadcast_to(jnp.sum(v[r, :], axis=1, keepdims=True), (ROWS, 128))
    second_product(k, v, sums, 0)
    at = k.shape[0]
    for copy, part in zip(copies, held):
        copy.wait()
        second_product(part, v, sums, at)
        at += part.shape[0]
    copies_out = out.shape[1]
    for i in range(place_ref.shape[0]):
        for h in range(2):
            row = sums[2 * i + h]
            for j in range(copies_out):
                out[place_ref[i], j, :, h * UNIT : (h + 1) * UNIT] = row


def second_product(k_ref, v_ref, sums, at):
    group = 2
    rows = v_ref.shape[0]
    lanes = [slice(t, t + 128) for t in range(0, UNIT, 128)]

    @pl.loop(0, k_ref.shape[0] // group)
    def _(j):
        total = [[jnp.zeros((8, 128), F32) for _ in lanes] for _ in range(group)]
        for q in range(0, rows, 8):
            v = v_ref[q : q + 8, :]
            for u in range(group):
                for t, c in enumerate(lanes):
                    total[u][t] = total[u][t] + k_ref[j * group + u, q : q + 8, c] * v
        for u in range(group):
            for t, c in enumerate(lanes):
                sums[at + j * group + u, :, c] = jnp.sum(total[u][t], axis=0, keepdims=True)


def prepared_scratch(n, width):
    return [
        pltpu.VMEM((n, width, UNIT), BF16),
        pltpu.VMEM((n, 2 * width, UNIT), F8),
        pltpu.VMEM((n, 1, UNIT), F32),
        pltpu.VMEM((n, 1, UNIT), F32),
    ]


def cost(rows, n, width):
    return pl.CostEstimate(
        flops=8 * rows * n * UNIT * width, bytes_accessed=rows * n * UNIT * 4, transcendentals=rows * n * UNIT
    )


def of(shape, dtype=F32):
    return jax.ShapeDtypeStruct(shape, dtype)


def count(blocks):
    return sum(b.shape[0] for b in blocks)


def opening(x, blocks):
    rows, width = x.shape
    n = count(blocks)
    return pl.pallas_call(
        opening_kernel,
        in_specs=[VMEM] * 3,
        out_specs=[VMEM] * 4 + [HBM],
        out_shape=[of((rows, width), BF16), of((rows, 2 * width), F8), of((rows, 128)), of((rows, 128)), of((n, rows, UNIT))],
        scratch_shapes=[pltpu.VMEM((n, rows, UNIT), F32), *prepared_scratch(n, width), pltpu.SemaphoreType.DMA],
        cost_estimate=cost(rows, n, width),
        compiler_params=pltpu.CompilerParams(vmem_limit_bytes=58 << 20),
        name="opening",
    )(x, *blocks)


def middle(group, xh, x8, a, v, blocks):
    rows, width = xh.shape
    n = count(blocks)
    return pl.pallas_call(
        functools.partial(middle_kernel, len(blocks), group),
        in_specs=[VMEM] * (4 + len(blocks)),
        out_specs=[VMEM, HBM],
        out_shape=[of((rows, 128)), of((n, rows, UNIT))],
        scratch_shapes=[pltpu.VMEM((n, rows, UNIT), F32), *prepared_scratch(n, width), pltpu.SemaphoreType.DMA],
        cost_estimate=cost(rows, n, width),
        compiler_params=pltpu.CompilerParams(vmem_limit_bytes=40 << 20),
        name="middle",
    )(xh, x8, a, v, *blocks)


def closing(group, place, copies, xh, x8, a, v, blocks, saved):
    rows, width = xh.shape
    n = count(blocks)
    total = n + count(saved)
    return pl.pallas_call(
        functools.partial(closing_kernel, len(blocks), len(saved), group),
        in_specs=[pl.BlockSpec(memory_space=pltpu.SMEM)] + [VMEM] * (4 + len(blocks)) + [HBM] * len(saved),
        out_specs=VMEM,
        out_shape=of((total // 2, copies, 1, 2 * UNIT)),
        scratch_shapes=[
            pltpu.VMEM((rows, 128), F32),
            pltpu.VMEM((total, 1, UNIT), F32),
            pltpu.VMEM((n, rows, UNIT), F32),
            *prepared_scratch(n, width),
            *[pltpu.VMEM(k.shape, F32) for k in saved],
            pltpu.SemaphoreType.DMA((len(saved),)),
        ],
        cost_estimate=cost(rows, 2 * n, width),
        compiler_params=pltpu.CompilerParams(vmem_limit_bytes=60 << 20),
        name="closing",
    )(place, xh, x8, a, v, *blocks, *saved)


RING, PAIR, CORES = 4, 2, 2


def index(x, z, core):
    return ((x % RING) * PAIR + z % PAIR) * CORES + core % CORES


def fetch(array, x=0, z=0, core=0):
    pairs = [
        (index(i + x, j + z, k + core), index(i, j, k))
        for i in range(RING)
        for j in range(PAIR)
        for k in range(CORES)
    ]
    return lax.ppermute(array, "blk", pairs)


def body(points, centres, coefficients):
    rows_size = lax.axis_size("rows")
    width = centres.shape[1]
    total_points = points.shape[0] * lax.axis_size("blk") * rows_size
    units = centres.shape[0] // UNIT
    own = jnp.concatenate(
        [
            centres.reshape(units, UNIT, width),
            coefficients.reshape(units, 1, UNIT),
            jnp.zeros((units, PACKED - UNIT - 1, width), F32),
        ],
        axis=1,
    )
    me = lax.axis_index("blk")
    at_x, at_z, at_core = me // (PAIR * CORES), me // CORES % PAIR, me % CORES

    def place(x, z, core):
        return index(at_x + x, at_z + z, at_core + core)

    def other(array):
        return fetch(array, core=1)

    after = lax.optimization_barrier
    near = [fetch(own, x=1), fetch(own, x=-1), fetch(own, z=1)]
    beside = other(own)
    xh, x8, a, v, k0 = opening(points, [own, beside])
    *near, v = after((*near, v))
    up, down, across = near
    near_other = [other(b) for b in near]
    far = [fetch(up, x=1), fetch(across, x=-1), fetch(up, z=1)]
    v, k1 = middle(4, xh, x8, a, v, near + near_other)
    *far, v = after((*far, v))
    far_other = [other(b) for b in far]
    last = [fetch(far[2][0:1], x=1), fetch(far[1][1:2], x=-1)]
    v, k2 = middle(3, xh, x8, a, v, far)
    *last, v = after((*last, v))
    last_other = [other(b) for b in last]
    order = [(2, 0, 1), (-1, 1, 1), (1, 1, 1), (2, 1, 0), (2, 1, 1)]
    order += [(0, 0, 0), (0, 0, 1)]
    order += [(1, 0, 0), (-1, 0, 0), (0, 1, 0), (1, 0, 1), (-1, 0, 1), (0, 1, 1)]
    order += [(2, 0, 0), (-1, 1, 0), (1, 1, 0)]
    places = jnp.stack([place(*o) for o in order]).astype(jnp.int32)
    sums = closing(5, places, rows_size, xh, x8, a, v, far_other + last + last_other, [k0, k1, k2])
    parts = lax.all_to_all(sums.reshape(-1, 1, 2 * UNIT), ("blk", "rows"), 0, 0, tiled=True)
    return jnp.sum(parts, axis=(0, 1)) / total_points


def solution(mesh):
    return jax.shard_map(
        body,
        mesh=mesh,
        in_specs=(P(("blk", "rows"), None), P("blk", None), P("blk")),
        out_specs=P("blk"),
        check_vma=False,
    )
```

```python
import functools
import math

import jax
import jax.numpy as jnp
from jax import lax
from jax.experimental import pallas as pl
from jax.experimental.pallas import tpu as pltpu
from jax.sharding import PartitionSpec as P

F32, BF16, F8 = jnp.float32, jnp.bfloat16, jnp.float8_e4m3fn
LOG2E = 1.4426950408889634
UNIT = 256
PACKED = 264
LIFT = 256.0
GRANT = 35 << 20
ROWS = 256
VMEM = pl.BlockSpec(memory_space=pltpu.VMEM)
ANY = pl.BlockSpec(memory_space=pl.ANY)
HBM = pl.BlockSpec(memory_space=pltpu.HBM)


def constants(width):
    scale = LOG2E / math.sqrt(width)
    return scale, 0.5 * LOG2E * math.sqrt(width)


def prepare_points(x_ref, xh_ref, x8_ref, a_ref):
    scale, offset = constants(x_ref.shape[1])
    for q in range(0, x_ref.shape[0], ROWS):
        r = slice(q, q + ROWS)
        x = x_ref[r, :]
        high = x.astype(BF16)
        low = (x - high.astype(F32)) * LIFT
        xh_ref[r, :] = high
        x8_ref[r, :] = jnp.concatenate([x.astype(F8), low.astype(F8)], axis=1)
        a = jnp.sum(x * x, axis=1, keepdims=True) * (-0.5 * scale) + offset
        a_ref[r, :] = jnp.broadcast_to(a, (ROWS, 128))


def prepare_units(refs, wh_ref, w8_ref, b_ref, c_ref):
    i = 0
    for ref in refs:
        for j in range(ref.shape[0]):
            width = ref.shape[2]
            scale, offset = constants(width)
            t = ref[j, 0:UNIT, :].T
            scaled = t * scale
            high = scaled.astype(BF16)
            low = (scaled - high.astype(F32)) * (LIFT / scale)
            wh_ref[i] = high
            w8_ref[i] = jnp.concatenate([low.astype(F8), t.astype(F8)], axis=0)
            b_ref[i] = jnp.sum(t * t, axis=0, keepdims=True) * (-0.5 * scale) + offset
            c_ref[i] = ref[j, UNIT : UNIT + 1, :]
            i += 1


def tile(i, r, xh_ref, x8_ref, a_ref, wh_ref, w8_ref, b_ref, c_ref, k_ref):
    scale, _ = constants(xh_ref.shape[1])
    main = jnp.dot(xh_ref[r, :], wh_ref[i], preferred_element_type=F32)
    cross = jnp.dot(x8_ref[r, :], w8_ref[i], preferred_element_type=F32)
    a = a_ref[r, :]
    value = None
    for t in range(0, UNIT, 128):
        c = slice(t, t + 128)
        k = jnp.exp2(main[:, c] + cross[:, c] * (scale / LIFT) + a + b_ref[i, :, c])
        k_ref[i, r, c] = k
        term = k * c_ref[i, :, c]
        value = term if value is None else value + term
    return value


def first_product(group, points, prepared, v_in, v_ref, k_ref, saved=None, sem=None):
    units = k_ref.shape[0]
    assert units % group == 0

    def save(j, q):
        part = (pl.ds(j * group, group), pl.ds(q, ROWS))
        return pltpu.make_async_copy(k_ref.at[part], saved.at[part], sem)

    @pl.loop(0, units // group)
    def _(j):
        for q in range(0, points[0].shape[0], ROWS):
            r = slice(q, q + ROWS)
            value = None
            for u in range(group):
                term = tile(j * group + u, r, *points, *prepared, k_ref)
                value = term if value is None else value + term
            before = 0.0 if v_in is None else v_in[r, :]
            v_ref[r, :] = jnp.where(j == 0, before, v_ref[r, :]) + value
            if saved is not None:
                save(j, q).start()

    if saved is not None:
        pltpu.make_async_copy(k_ref, saved, sem).wait()


def opening_kernel(group, x_ref, *rest):
    units, (xh, x8, a, v, k), prepared = rest[:2], rest[2:7], rest[7:]
    prepare_points(x_ref, xh, x8, a)
    prepare_units(units, *prepared)
    v[...] = jnp.zeros_like(v)
    first_product(group, (xh, x8, a), prepared, None, v, k)


def load(sources, targets, sem):
    copies = [pltpu.make_async_copy(f, t, sem.at[i]) for i, (f, t) in enumerate(zip(sources, targets))]
    for copy in copies:
        copy.start()
    return copies


def middle_kernel(n, group, *rest):
    sources, units, (v, saved), scratch = rest[:4], rest[4 : 4 + n], rest[4 + n : 6 + n], rest[6 + n :]
    (xh, x8, a, v_in), prepared, sem = scratch[:4], scratch[4:8], scratch[8]
    copies = load(sources, scratch[:4], sem)
    prepare_units(units, *prepared)
    for copy in copies:
        copy.wait()
    v[...] = v_in[...]
    if len(scratch) > 9:
        k, save_sem = scratch[9:]
        first_product(group, (xh, x8, a), prepared, v_in, v, k, saved, save_sem)
    else:
        first_product(group, (xh, x8, a), prepared, v_in, v, saved)


def closing_kernel(n, m, f, group, place_ref, *rest):
    sources, units, kept, saved = rest[:4], rest[4 : 4 + n], rest[4 + n : 4 + n + m], rest[4 + n + m : 4 + n + m + f]
    out, xh, x8, a, v_in, v, sums, k, *prepared, held, points_sem, sem = rest[4 + n + m + f :]
    copies = load(sources, (xh, x8, a, v_in), points_sem)
    (saved,) = saved
    early = held.shape[0]
    late = saved.shape[0] - early
    fetch = pltpu.make_async_copy(saved.at[0:early], held, sem.at[0])
    fetch_late = pltpu.make_async_copy(saved.at[early:], k.at[0:late], sem.at[1])
    prepare_units(units, *prepared)
    for copy in copies:
        copy.wait()
    fetch.start()
    v[...] = v_in[...]
    first_product(group, (xh, x8, a), prepared, v_in, v, k)
    for q in range(0, v.shape[0], ROWS):
        r = slice(q, q + ROWS)
        v[r, :] = jnp.broadcast_to(jnp.sum(v[r, :], axis=1, keepdims=True), (ROWS, 128))
    second_product(k, v, sums, 0)
    fetch_late.start()
    at = k.shape[0]
    for part in kept:
        second_product(part, v, sums, at)
        at += part.shape[0]
    fetch.wait()
    second_product(held, v, sums, at)
    fetch_late.wait()
    second_product(k.at[0:late], v, sums, at + early)
    for i in range(place_ref.shape[0]):
        for h in range(2):
            row = sums[2 * i + h]
            for j in range(out.shape[1]):
                out[place_ref[i], j, :, h * UNIT : (h + 1) * UNIT] = row


def second_product(k_ref, v_ref, sums, at):
    units, rows = k_ref.shape[:2]
    group = next(g for g in (5, 4, 3, 2, 1) if units % g == 0)
    lanes = [slice(t, t + 128) for t in range(0, UNIT, 128)]

    @pl.loop(0, units // group)
    def _(j):
        total = {}
        for q in range(0, rows, 8):
            v = v_ref[q : q + 8, :]
            for u in range(group):
                for t, c in enumerate(lanes):
                    term = k_ref[j * group + u, q : q + 8, c] * v
                    total[u, t] = total[u, t] + term if q else term
        for u in range(group):
            for t, c in enumerate(lanes):
                sums[at + j * group + u, :, c] = jnp.sum(total[u, t], axis=0, keepdims=True)


def points_scratch(rows, width):
    return [pltpu.VMEM(s, d) for s, d in (((rows, width), BF16), ((rows, 2 * width), F8), ((rows, 128), F32), ((rows, 128), F32))]


def prepared_scratch(n, width):
    return [
        pltpu.VMEM((n, width, UNIT), BF16),
        pltpu.VMEM((n, 2 * width, UNIT), F8),
        pltpu.VMEM((n, 1, UNIT), F32),
        pltpu.VMEM((n, 1, UNIT), F32),
    ]


def cost(rows, n, width):
    return pl.CostEstimate(
        flops=8 * rows * n * UNIT * width, bytes_accessed=rows * n * UNIT * 4, transcendentals=rows * n * UNIT
    )


def of(shape, dtype=F32):
    return jax.ShapeDtypeStruct(shape, dtype)


def count(blocks):
    return sum(b.shape[0] for b in blocks)


def opening(group, x, blocks):
    rows, width = x.shape
    n = count(blocks)
    return pl.pallas_call(
        functools.partial(opening_kernel, group),
        in_specs=[VMEM] * 3,
        out_specs=[VMEM] * 5,
        out_shape=[of((rows, width), BF16), of((rows, 2 * width), F8), of((rows, 128)), of((rows, 128)), pltpu.VMEM((n, rows, UNIT), F32)],
        scratch_shapes=prepared_scratch(n, width),
        cost_estimate=cost(rows, n, width),
        compiler_params=pltpu.CompilerParams(vmem_limit_bytes=GRANT),
        name="opening",
    )(x, *blocks)


def middle(group, xh, x8, a, v, blocks, keep):
    rows, width = xh.shape
    n = count(blocks)
    return pl.pallas_call(
        functools.partial(middle_kernel, len(blocks), group),
        in_specs=[ANY] * 4 + [VMEM] * len(blocks),
        out_specs=[VMEM, VMEM if keep else HBM],
        out_shape=[of((rows, 128)), (pltpu.VMEM((n, rows, UNIT), F32) if keep else of((n, rows, UNIT)))],
        scratch_shapes=[
            *points_scratch(rows, width),
            *prepared_scratch(n, width),
            pltpu.SemaphoreType.DMA((4,)),
            *([] if keep else [pltpu.VMEM((n, rows, UNIT), F32), pltpu.SemaphoreType.DMA]),
        ],
        cost_estimate=cost(rows, n, width),
        compiler_params=pltpu.CompilerParams(vmem_limit_bytes=GRANT),
        name="middle",
    )(xh, x8, a, v, *blocks)


def closing(group, early, place, copies, xh, x8, a, v, blocks, kept, saved):
    rows, width = xh.shape
    n = count(blocks)
    total = n + count(kept) + count(saved)
    return pl.pallas_call(
        functools.partial(closing_kernel, len(blocks), len(kept), len(saved), group),
        in_specs=[pl.BlockSpec(memory_space=pltpu.SMEM)] + [ANY] * 4 + [VMEM] * (len(blocks) + len(kept)) + [HBM] * len(saved),
        out_specs=VMEM,
        out_shape=of((total // 2, copies, 1, 2 * UNIT)),
        scratch_shapes=[
            *points_scratch(rows, width),
            pltpu.VMEM((rows, 128), F32),
            pltpu.VMEM((total, 1, UNIT), F32),
            pltpu.VMEM((n, rows, UNIT), F32),
            *prepared_scratch(n, width),
            pltpu.VMEM((early, rows, UNIT), F32),
            pltpu.SemaphoreType.DMA((4,)),
            pltpu.SemaphoreType.DMA((2,)),
        ],
        cost_estimate=cost(rows, 2 * n, width),
        compiler_params=pltpu.CompilerParams(vmem_limit_bytes=GRANT),
        name="closing",
    )(place, xh, x8, a, v, *blocks, *[pltpu.with_memory_space_constraint(k, pltpu.VMEM) for k in kept], *saved)


RING, PAIR, CORES = 4, 2, 2


def index(x, z, core):
    return ((x % RING) * PAIR + z % PAIR) * CORES + core % CORES


def fetch(array, x=0, z=0, core=0):
    pairs = [
        (index(i + x, j + z, k + core), index(i, j, k))
        for i in range(RING)
        for j in range(PAIR)
        for k in range(CORES)
    ]
    return lax.ppermute(array, "blk", pairs)


def body(points, centres, coefficients):
    rows_size = lax.axis_size("rows")
    width = centres.shape[1]
    total_points = points.shape[0] * lax.axis_size("blk") * rows_size
    units = centres.shape[0] // UNIT
    own = jnp.concatenate(
        [
            centres.reshape(units, UNIT, width),
            coefficients.reshape(units, 1, UNIT),
            jnp.zeros((units, PACKED - UNIT - 1, width), F32),
        ],
        axis=1,
    )
    me = lax.axis_index("blk")
    at_x, at_z, at_core = me // (PAIR * CORES), me // CORES % PAIR, me % CORES

    def place(x, z, core):
        return index(at_x + x, at_z + z, at_core + core)

    def other(array):
        return fetch(array, core=1)

    order = [(2, 0, 1), (-1, 1, 1), (1, 1, 1), (2, 1, 0), (2, 1, 1)]
    order += [(0, 0, 0), (0, 0, 1)]
    order += [(2, 0, 0), (-1, 1, 0), (1, 1, 0)]
    order += [(1, 0, 0), (-1, 0, 0), (0, 1, 0), (1, 0, 1), (-1, 0, 1), (0, 1, 1)]
    places = jnp.stack([place(*o) for o in order]).astype(jnp.int32)
    after = lax.optimization_barrier
    near = [fetch(own, x=1), fetch(own, x=-1), fetch(own, z=1)]
    beside = other(own)
    xh, x8, a, v, k0 = opening(2, points, [own, beside])
    *near, v, places = after((*near, v, places))
    up, down, across = near
    far = [fetch(up, x=1), fetch(across, x=-1), fetch(up, z=1)]
    near_other = [other(b) for b in near]
    v, k1 = middle(4, xh, x8, a, v, near + near_other, False)
    *far, v = after((*far, v))
    last = [fetch(far[2][0:1], x=1), fetch(far[1][1:2], x=-1)]
    far_other = [other(b) for b in far]
    v, k2 = middle(3, xh, x8, a, v, far, True)
    *last, v = after((*last, v))
    last_other = [other(b) for b in last]
    sums = closing(10, 8, places, rows_size, xh, x8, a, v, far_other + last + last_other, [k0, k2], [k1])
    parts = lax.all_to_all(sums.reshape(-1, 1, 2 * UNIT), ("blk", "rows"), 0, 0, tiled=True)
    return jnp.sum(parts, axis=(0, 1)) / total_points


def solution(mesh):
    return jax.shard_map(
        body,
        mesh=mesh,
        in_specs=(P(("blk", "rows"), None), P("blk", None), P("blk")),
        out_specs=P("blk"),
        check_vma=False,
    )
```

```python
import functools
import math

import jax
import jax.numpy as jnp
from jax import lax
from jax.experimental import pallas as pl
from jax.experimental.pallas import tpu as pltpu
from jax.sharding import PartitionSpec as P

F32, BF16, F8 = jnp.float32, jnp.bfloat16, jnp.float8_e4m3fn
LOG2E = 1.4426950408889634
UNIT = 256
PACKED = 264
LIFT = 256.0
GRANT = 35 << 20
ROWS = 256
VMEM = pl.BlockSpec(memory_space=pltpu.VMEM)
ANY = pl.BlockSpec(memory_space=pl.ANY)
HBM = pl.BlockSpec(memory_space=pltpu.HBM)


def constants(width):
    scale = LOG2E / math.sqrt(width)
    return scale, 0.5 * LOG2E * math.sqrt(width)


def prepare_points(x_ref, xh_ref, x8_ref, a_ref):
    scale, offset = constants(x_ref.shape[1])
    for q in range(0, x_ref.shape[0], ROWS):
        r = slice(q, q + ROWS)
        x = x_ref[r, :]
        high = x.astype(BF16)
        low = (x - high.astype(F32)) * LIFT
        xh_ref[r, :] = high
        x8_ref[r, :] = jnp.concatenate([x.astype(F8), low.astype(F8)], axis=1)
        a = jnp.sum(x * x, axis=1, keepdims=True) * (-0.5 * scale) + offset
        a_ref[r, :] = jnp.broadcast_to(a, (ROWS, 128))


def prepare_units(refs, wh_ref, w8_ref, b_ref, c_ref):
    i = 0
    for ref in refs:
        for j in range(ref.shape[0]):
            width = ref.shape[2]
            scale, offset = constants(width)
            t = ref[j, 0:UNIT, :].T
            scaled = t * scale
            high = scaled.astype(BF16)
            low = (scaled - high.astype(F32)) * (LIFT / scale)
            wh_ref[i] = high
            w8_ref[i] = jnp.concatenate([low.astype(F8), t.astype(F8)], axis=0)
            b_ref[i] = jnp.sum(t * t, axis=0, keepdims=True) * (-0.5 * scale) + offset
            c_ref[i] = ref[j, UNIT : UNIT + 1, :]
            i += 1


def tile(i, r, xh_ref, x8_ref, a_ref, wh_ref, w8_ref, b_ref, c_ref, k_ref):
    scale, _ = constants(xh_ref.shape[1])
    main = jnp.dot(xh_ref[r, :], wh_ref[i], preferred_element_type=F32)
    cross = jnp.dot(x8_ref[r, :], w8_ref[i], preferred_element_type=F32)
    a = a_ref[r, :]
    value = None
    for t in range(0, UNIT, 128):
        c = slice(t, t + 128)
        k = jnp.exp2(main[:, c] + cross[:, c] * (scale / LIFT) + a + b_ref[i, :, c])
        k_ref[i, r, c] = k
        term = k * c_ref[i, :, c]
        value = term if value is None else value + term
    return value


def first_product(group, points, prepared, v_in, v_ref, k_ref, saved=None, sem=None):
    units = k_ref.shape[0]
    assert units % group == 0

    def save(j, q):
        part = (pl.ds(j * group, group), pl.ds(q, ROWS))
        return pltpu.make_async_copy(k_ref.at[part], saved.at[part], sem)

    @pl.loop(0, units // group)
    def _(j):
        for q in range(0, points[0].shape[0], ROWS):
            r = slice(q, q + ROWS)
            value = None
            for u in range(group):
                term = tile(j * group + u, r, *points, *prepared, k_ref)
                value = term if value is None else value + term
            before = 0.0 if v_in is None else v_in[r, :]
            v_ref[r, :] = jnp.where(j == 0, before, v_ref[r, :]) + value
            if saved is not None:
                save(j, q).start()

    if saved is not None:
        pltpu.make_async_copy(k_ref, saved, sem).wait()


def opening_kernel(group, x_ref, *rest):
    units, (xh, x8, a, v, k), prepared = rest[:2], rest[2:7], rest[7:]
    prepare_points(x_ref, xh, x8, a)
    prepare_units(units, *prepared)
    v[...] = jnp.zeros_like(v)
    first_product(group, (xh, x8, a), prepared, None, v, k)


def load(sources, targets, sem):
    copies = [pltpu.make_async_copy(f, t, sem.at[i]) for i, (f, t) in enumerate(zip(sources, targets))]
    for copy in copies:
        copy.start()
    return copies


def middle_kernel(n, group, *rest):
    sources, units, (v, saved), scratch = rest[:4], rest[4 : 4 + n], rest[4 + n : 6 + n], rest[6 + n :]
    (xh, x8, a, v_in), prepared, sem = scratch[:4], scratch[4:8], scratch[8]
    copies = load(sources, scratch[:4], sem)
    prepare_units(units, *prepared)
    for copy in copies:
        copy.wait()
    v[...] = v_in[...]
    if len(scratch) > 9:
        k, save_sem = scratch[9:]
        first_product(group, (xh, x8, a), prepared, v_in, v, k, saved, save_sem)
    else:
        first_product(group, (xh, x8, a), prepared, v_in, v, saved)


def closing_kernel(n, m, f, group, place_ref, *rest):
    sources, units, kept, saved = rest[:4], rest[4 : 4 + n], rest[4 + n : 4 + n + m], rest[4 + n + m : 4 + n + m + f]
    out, xh, x8, a, v_in, v, sums, k, *prepared, held, points_sem, sem = rest[4 + n + m + f :]
    copies = load(sources, (xh, x8, a, v_in), points_sem)
    (saved,) = saved
    early = held.shape[0]
    late = saved.shape[0] - early
    fetch = pltpu.make_async_copy(saved.at[0:early], held, sem.at[0])
    fetch_late = pltpu.make_async_copy(saved.at[early:], k.at[0:late], sem.at[1])
    prepare_units(units, *prepared)
    for copy in copies:
        copy.wait()
    fetch.start()
    v[...] = v_in[...]
    first_product(group, (xh, x8, a), prepared, v_in, v, k)
    for q in range(0, v.shape[0], ROWS):
        r = slice(q, q + ROWS)
        v[r, :] = jnp.broadcast_to(jnp.sum(v[r, :], axis=1, keepdims=True), (ROWS, 128))
    second_product(k, v, sums, 0)
    fetch_late.start()
    at = k.shape[0]
    for part in kept:
        second_product(part, v, sums, at)
        at += part.shape[0]
    fetch.wait()
    second_product(held, v, sums, at)
    fetch_late.wait()
    second_product(k.at[0:late], v, sums, at + early)
    for i in range(place_ref.shape[0]):
        for h in range(2):
            row = sums[2 * i + h]
            for j in range(out.shape[1]):
                out[place_ref[i], j, :, h * UNIT : (h + 1) * UNIT] = row


def second_product(k_ref, v_ref, sums, at):
    units, rows = k_ref.shape[:2]
    group = next(g for g in (5, 4, 3, 2, 1) if units % g == 0)
    lanes = [slice(t, t + 128) for t in range(0, UNIT, 128)]

    @pl.loop(0, units // group)
    def _(j):
        total = {}
        for q in range(0, rows, 8):
            v = v_ref[q : q + 8, :]
            for u in range(group):
                for t, c in enumerate(lanes):
                    term = k_ref[j * group + u, q : q + 8, c] * v
                    total[u, t] = total[u, t] + term if q else term
        for u in range(group):
            for t, c in enumerate(lanes):
                sums[at + j * group + u, :, c] = jnp.sum(total[u, t], axis=0, keepdims=True)


def points_scratch(rows, width):
    return [pltpu.VMEM(s, d) for s, d in (((rows, width), BF16), ((rows, 2 * width), F8), ((rows, 128), F32), ((rows, 128), F32))]


def prepared_scratch(n, width):
    return [
        pltpu.VMEM((n, width, UNIT), BF16),
        pltpu.VMEM((n, 2 * width, UNIT), F8),
        pltpu.VMEM((n, 1, UNIT), F32),
        pltpu.VMEM((n, 1, UNIT), F32),
    ]


def cost(rows, n, width):
    return pl.CostEstimate(
        flops=rows * width, bytes_accessed=rows * width, transcendentals=rows
    )


def of(shape, dtype=F32):
    return jax.ShapeDtypeStruct(shape, dtype)


def count(blocks):
    return sum(b.shape[0] for b in blocks)


def opening(group, x, blocks):
    rows, width = x.shape
    n = count(blocks)
    return pl.pallas_call(
        functools.partial(opening_kernel, group),
        in_specs=[VMEM] * 3,
        out_specs=[VMEM] * 5,
        out_shape=[of((rows, width), BF16), of((rows, 2 * width), F8), of((rows, 128)), of((rows, 128)), pltpu.VMEM((n, rows, UNIT), F32)],
        scratch_shapes=prepared_scratch(n, width),
        cost_estimate=cost(rows, n, width),
        compiler_params=pltpu.CompilerParams(vmem_limit_bytes=GRANT),
        name="opening",
    )(x, *blocks)


def middle(group, xh, x8, a, v, blocks, keep):
    rows, width = xh.shape
    n = count(blocks)
    return pl.pallas_call(
        functools.partial(middle_kernel, len(blocks), group),
        in_specs=[ANY] * 4 + [VMEM] * len(blocks),
        out_specs=[VMEM, VMEM if keep else HBM],
        out_shape=[of((rows, 128)), (pltpu.VMEM((n, rows, UNIT), F32) if keep else of((n, rows, UNIT)))],
        scratch_shapes=[
            *points_scratch(rows, width),
            *prepared_scratch(n, width),
            pltpu.SemaphoreType.DMA((4,)),
            *([] if keep else [pltpu.VMEM((n, rows, UNIT), F32), pltpu.SemaphoreType.DMA]),
        ],
        cost_estimate=cost(rows, n, width),
        compiler_params=pltpu.CompilerParams(vmem_limit_bytes=GRANT),
        name="middle",
    )(xh, x8, a, v, *blocks)


def closing(group, early, place, copies, xh, x8, a, v, blocks, kept, saved):
    rows, width = xh.shape
    n = count(blocks)
    total = n + count(kept) + count(saved)
    return pl.pallas_call(
        functools.partial(closing_kernel, len(blocks), len(kept), len(saved), group),
        in_specs=[pl.BlockSpec(memory_space=pltpu.SMEM)] + [ANY] * 4 + [VMEM] * (len(blocks) + len(kept)) + [HBM] * len(saved),
        out_specs=VMEM,
        out_shape=of((total // 2, copies, 1, 2 * UNIT)),
        scratch_shapes=[
            *points_scratch(rows, width),
            pltpu.VMEM((rows, 128), F32),
            pltpu.VMEM((total, 1, UNIT), F32),
            pltpu.VMEM((n, rows, UNIT), F32),
            *prepared_scratch(n, width),
            pltpu.VMEM((early, rows, UNIT), F32),
            pltpu.SemaphoreType.DMA((4,)),
            pltpu.SemaphoreType.DMA((2,)),
        ],
        cost_estimate=cost(rows, 2 * n, width),
        compiler_params=pltpu.CompilerParams(vmem_limit_bytes=GRANT),
        name="closing",
    )(place, xh, x8, a, v, *blocks, *[pltpu.with_memory_space_constraint(k, pltpu.VMEM) for k in kept], *saved)


RING, PAIR, CORES = 4, 2, 2


def index(x, z, core):
    return ((x % RING) * PAIR + z % PAIR) * CORES + core % CORES


def fetch(array, x=0, z=0, core=0):
    pairs = [
        (index(i + x, j + z, k + core), index(i, j, k))
        for i in range(RING)
        for j in range(PAIR)
        for k in range(CORES)
    ]
    return lax.ppermute(array, "blk", pairs)


def body(points, centres, coefficients):
    rows_size = lax.axis_size("rows")
    width = centres.shape[1]
    total_points = points.shape[0] * lax.axis_size("blk") * rows_size
    units = centres.shape[0] // UNIT
    own = jnp.concatenate(
        [
            centres.reshape(units, UNIT, width),
            coefficients.reshape(units, 1, UNIT),
            jnp.zeros((units, PACKED - UNIT - 1, width), F32),
        ],
        axis=1,
    )
    me = lax.axis_index("blk")
    at_x, at_z, at_core = me // (PAIR * CORES), me // CORES % PAIR, me % CORES

    def place(x, z, core):
        return index(at_x + x, at_z + z, at_core + core)

    def other(array):
        return fetch(array, core=1)

    order = [(2, 0, 1), (-1, 1, 1), (1, 1, 1), (2, 1, 0), (2, 1, 1)]
    order += [(0, 0, 0), (0, 0, 1)]
    order += [(2, 0, 0), (-1, 1, 0), (1, 1, 0)]
    order += [(1, 0, 0), (-1, 0, 0), (0, 1, 0), (1, 0, 1), (-1, 0, 1), (0, 1, 1)]
    places = jnp.stack([place(*o) for o in order]).astype(jnp.int32)
    after = lax.optimization_barrier
    near = [fetch(own, x=1), fetch(own, x=-1), fetch(own, z=1)]
    beside = other(own)
    xh, x8, a, v, k0 = opening(2, points, [own, beside])
    *near, v, places = after((*near, v, places))
    up, down, across = near
    far = [fetch(up, x=1), fetch(across, x=-1), fetch(up, z=1)]
    near_other = [other(b) for b in near]
    v, k1 = middle(4, xh, x8, a, v, near + near_other, False)
    *far, v = after((*far, v))
    last = [fetch(far[2][0:1], x=1), fetch(far[1][1:2], x=-1)]
    far_other = [other(b) for b in far]
    v, k2 = middle(3, xh, x8, a, v, far, True)
    *last, v = after((*last, v))
    last_other = [other(b) for b in last]
    sums = closing(10, 8, places, rows_size, xh, x8, a, v, far_other + last + last_other, [k0, k2], [k1])
    parts = lax.all_to_all(sums.reshape(-1, 1, 2 * UNIT), ("blk", "rows"), 0, 0, tiled=True)
    return jnp.sum(parts, axis=(0, 1)) / total_points


def solution(mesh):
    return jax.shard_map(
        body,
        mesh=mesh,
        in_specs=(P(("blk", "rows"), None), P("blk", None), P("blk")),
        out_specs=P("blk"),
        check_vma=False,
    )
```

```python
import functools
import math

import jax
import jax.numpy as jnp
from jax import lax
from jax.experimental import pallas as pl
from jax.experimental.pallas import tpu as pltpu
from jax.sharding import PartitionSpec as P

F32, BF16, F8 = jnp.float32, jnp.bfloat16, jnp.float8_e4m3fn
LOG2E = 1.4426950408889634
UNIT = 256
PACKED = 264
LIFT = 256.0
GRANT = 35 << 20
ROWS = 256
VMEM = pl.BlockSpec(memory_space=pltpu.VMEM)
ANY = pl.BlockSpec(memory_space=pl.ANY)
HBM = pl.BlockSpec(memory_space=pltpu.HBM)


def constants(width):
    scale = LOG2E / math.sqrt(width)
    return scale, 0.5 * LOG2E * math.sqrt(width)


def prepare_points(x_ref, xh_ref, x8_ref, a_ref):
    scale, offset = constants(x_ref.shape[1])
    for q in range(0, x_ref.shape[0], ROWS):
        r = slice(q, q + ROWS)
        x = x_ref[r, :]
        high = x.astype(BF16)
        low = (x - high.astype(F32)) * LIFT
        xh_ref[r, :] = high
        x8_ref[r, :] = jnp.concatenate([x.astype(F8), low.astype(F8)], axis=1)
        a = jnp.sum(x * x, axis=1, keepdims=True) * (-0.5 * scale) + offset
        a_ref[r, :] = jnp.broadcast_to(a, (ROWS, 128))


def prepare_units(refs, wh_ref, w8_ref, b_ref, c_ref):
    i = 0
    for ref in refs:
        for j in range(ref.shape[0]):
            width = ref.shape[2]
            scale, offset = constants(width)
            t = ref[j, 0:UNIT, :].T
            scaled = t * scale
            high = scaled.astype(BF16)
            low = (scaled - high.astype(F32)) * (LIFT / scale)
            wh_ref[i] = high
            w8_ref[i] = jnp.concatenate([low.astype(F8), t.astype(F8)], axis=0)
            b_ref[i] = jnp.sum(t * t, axis=0, keepdims=True) * (-0.5 * scale) + offset
            c_ref[i] = ref[j, UNIT : UNIT + 1, :]
            i += 1


def tile(i, r, xh_ref, x8_ref, a_ref, wh_ref, w8_ref, b_ref, c_ref, k_ref):
    scale, _ = constants(xh_ref.shape[1])
    main = jnp.dot(xh_ref[r, :], wh_ref[i], preferred_element_type=F32)
    cross = jnp.dot(x8_ref[r, :], w8_ref[i], preferred_element_type=F32)
    a = a_ref[r, :]
    value = None
    for t in range(0, UNIT, 128):
        c = slice(t, t + 128)
        k = jnp.exp2(main[:, c] + cross[:, c] * (scale / LIFT) + a + b_ref[i, :, c])
        k_ref[i, r, c] = k
        term = k * c_ref[i, :, c]
        value = term if value is None else value + term
    return value


def first_product(group, points, prepared, v_in, v_ref, k_ref, saved=None, sem=None):
    units = k_ref.shape[0]
    assert units % group == 0

    def save(j, q):
        part = (pl.ds(j * group, group), pl.ds(q, ROWS))
        return pltpu.make_async_copy(k_ref.at[part], saved.at[part], sem)

    @pl.loop(0, units // group)
    def _(j):
        for q in range(0, points[0].shape[0], ROWS):
            r = slice(q, q + ROWS)
            value = None
            for u in range(group):
                term = tile(j * group + u, r, *points, *prepared, k_ref)
                value = term if value is None else value + term
            before = 0.0 if v_in is None else v_in[r, :]
            v_ref[r, :] = jnp.where(j == 0, before, v_ref[r, :]) + value
            if saved is not None:
                save(j, q).start()

    if saved is not None:
        pltpu.make_async_copy(k_ref, saved, sem).wait()


def opening_kernel(group, x_ref, *rest):
    units, (xh, x8, a, v, k), prepared = rest[:2], rest[2:7], rest[7:]
    prepare_points(x_ref, xh, x8, a)
    prepare_units(units, *prepared)
    v[...] = jnp.zeros_like(v)
    first_product(group, (xh, x8, a), prepared, None, v, k)


def load(sources, targets, sem):
    copies = [pltpu.make_async_copy(f, t, sem.at[i]) for i, (f, t) in enumerate(zip(sources, targets))]
    for copy in copies:
        copy.start()
    return copies


def middle_kernel(n, group, *rest):
    sources, units, (v, saved), scratch = rest[:4], rest[4 : 4 + n], rest[4 + n : 6 + n], rest[6 + n :]
    (xh, x8, a, v_in), prepared, sem = scratch[:4], scratch[4:8], scratch[8]
    copies = load(sources, scratch[:4], sem)
    prepare_units(units, *prepared)
    for copy in copies:
        copy.wait()
    v[...] = v_in[...]
    if len(scratch) > 9:
        k, save_sem = scratch[9:]
        first_product(group, (xh, x8, a), prepared, v_in, v, k, saved, save_sem)
    else:
        first_product(group, (xh, x8, a), prepared, v_in, v, saved)


def closing_kernel(n, m, f, group, place_ref, *rest):
    sources, v_in, units, kept, saved = rest[:3], rest[3], rest[4 : 4 + n], rest[4 + n : 4 + n + m], rest[4 + n + m : 4 + n + m + f]
    out, xh, x8, a, v, sums, k, *prepared, held, points_sem, sem = rest[4 + n + m + f :]
    copies = load(sources, (xh, x8, a), points_sem)
    (saved,) = saved
    early = held.shape[0]
    late = saved.shape[0] - early
    fetch = pltpu.make_async_copy(saved.at[0:early], held, sem.at[0])
    fetch_late = pltpu.make_async_copy(saved.at[early:], k.at[0:late], sem.at[1])
    prepare_units(units, *prepared)
    for copy in copies:
        copy.wait()
    fetch.start()
    v[...] = v_in[...]
    first_product(group, (xh, x8, a), prepared, v_in, v, k)
    for q in range(0, v.shape[0], ROWS):
        r = slice(q, q + ROWS)
        v[r, :] = jnp.broadcast_to(jnp.sum(v[r, :], axis=1, keepdims=True), (ROWS, 128))
    second_product(k, v, sums, 0)
    fetch_late.start()
    at = k.shape[0]
    for part in kept:
        second_product(part, v, sums, at)
        at += part.shape[0]
    fetch.wait()
    second_product(held, v, sums, at)
    fetch_late.wait()
    second_product(k.at[0:late], v, sums, at + early)
    for i in range(place_ref.shape[0]):
        for h in range(2):
            row = sums[2 * i + h]
            for j in range(out.shape[1]):
                out[place_ref[i], j, :, h * UNIT : (h + 1) * UNIT] = row


def second_product(k_ref, v_ref, sums, at):
    units, rows = k_ref.shape[:2]
    group = next(g for g in (5, 4, 3, 2, 1) if units % g == 0)
    lanes = [slice(t, t + 128) for t in range(0, UNIT, 128)]

    @pl.loop(0, units // group)
    def _(j):
        total = {}
        for q in range(0, rows, 8):
            v = v_ref[q : q + 8, :]
            for u in range(group):
                for t, c in enumerate(lanes):
                    term = k_ref[j * group + u, q : q + 8, c] * v
                    total[u, t] = total[u, t] + term if q else term
        for u in range(group):
            for t, c in enumerate(lanes):
                sums[at + j * group + u, :, c] = jnp.sum(total[u, t], axis=0, keepdims=True)


def points_scratch(rows, width):
    return [pltpu.VMEM(s, d) for s, d in (((rows, width), BF16), ((rows, 2 * width), F8), ((rows, 128), F32), ((rows, 128), F32))]


def prepared_scratch(n, width):
    return [
        pltpu.VMEM((n, width, UNIT), BF16),
        pltpu.VMEM((n, 2 * width, UNIT), F8),
        pltpu.VMEM((n, 1, UNIT), F32),
        pltpu.VMEM((n, 1, UNIT), F32),
    ]


def cost(rows, n, width):
    return pl.CostEstimate(
        flops=rows * width, bytes_accessed=rows * width, transcendentals=rows
    )


def of(shape, dtype=F32):
    return jax.ShapeDtypeStruct(shape, dtype)


def count(blocks):
    return sum(b.shape[0] for b in blocks)


def opening(group, x, blocks):
    rows, width = x.shape
    n = count(blocks)
    return pl.pallas_call(
        functools.partial(opening_kernel, group),
        in_specs=[VMEM] * 3,
        out_specs=[VMEM] * 5,
        out_shape=[of((rows, width), BF16), of((rows, 2 * width), F8), of((rows, 128)), of((rows, 128)), pltpu.VMEM((n, rows, UNIT), F32)],
        scratch_shapes=prepared_scratch(n, width),
        cost_estimate=cost(rows, n, width),
        compiler_params=pltpu.CompilerParams(vmem_limit_bytes=GRANT),
        name="opening",
    )(x, *blocks)


def middle(group, xh, x8, a, v, blocks, keep):
    rows, width = xh.shape
    n = count(blocks)
    return pl.pallas_call(
        functools.partial(middle_kernel, len(blocks), group),
        in_specs=[ANY] * 4 + [VMEM] * len(blocks),
        out_specs=[VMEM, VMEM if keep else HBM],
        out_shape=[pltpu.VMEM((rows, 128), F32) if keep else of((rows, 128)), (pltpu.VMEM((n, rows, UNIT), F32) if keep else of((n, rows, UNIT)))],
        scratch_shapes=[
            *points_scratch(rows, width),
            *prepared_scratch(n, width),
            pltpu.SemaphoreType.DMA((4,)),
            *([] if keep else [pltpu.VMEM((n, rows, UNIT), F32), pltpu.SemaphoreType.DMA]),
        ],
        cost_estimate=cost(rows, n, width),
        compiler_params=pltpu.CompilerParams(vmem_limit_bytes=GRANT),
        name="middle",
    )(xh, x8, a, v, *blocks)


def closing(group, early, place, copies, xh, x8, a, v, blocks, kept, saved):
    rows, width = xh.shape
    n = count(blocks)
    total = n + count(kept) + count(saved)
    return pl.pallas_call(
        functools.partial(closing_kernel, len(blocks), len(kept), len(saved), group),
        in_specs=[pl.BlockSpec(memory_space=pltpu.SMEM)] + [ANY] * 3 + [VMEM] * (1 + len(blocks) + len(kept)) + [HBM] * len(saved),
        out_specs=VMEM,
        out_shape=of((total // 2, copies, 1, 2 * UNIT)),
        scratch_shapes=[
            *points_scratch(rows, width)[:3],
            pltpu.VMEM((rows, 128), F32),
            pltpu.VMEM((total, 1, UNIT), F32),
            pltpu.VMEM((n, rows, UNIT), F32),
            *prepared_scratch(n, width),
            pltpu.VMEM((early, rows, UNIT), F32),
            pltpu.SemaphoreType.DMA((3,)),
            pltpu.SemaphoreType.DMA((2,)),
        ],
        cost_estimate=cost(rows, 2 * n, width),
        compiler_params=pltpu.CompilerParams(vmem_limit_bytes=GRANT),
        name="closing",
    )(place, xh, x8, a, pltpu.with_memory_space_constraint(v, pltpu.VMEM), *blocks, *[pltpu.with_memory_space_constraint(k, pltpu.VMEM) for k in kept], *saved)


RING, PAIR, CORES = 4, 2, 2


def index(x, z, core):
    return ((x % RING) * PAIR + z % PAIR) * CORES + core % CORES


def fetch(array, x=0, z=0, core=0):
    pairs = [
        (index(i + x, j + z, k + core), index(i, j, k))
        for i in range(RING)
        for j in range(PAIR)
        for k in range(CORES)
    ]
    return lax.ppermute(array, "blk", pairs)


def body(points, centres, coefficients):
    rows_size = lax.axis_size("rows")
    width = centres.shape[1]
    total_points = points.shape[0] * lax.axis_size("blk") * rows_size
    units = centres.shape[0] // UNIT
    own = jnp.concatenate(
        [
            centres.reshape(units, UNIT, width),
            coefficients.reshape(units, 1, UNIT),
            jnp.zeros((units, PACKED - UNIT - 1, width), F32),
        ],
        axis=1,
    )
    me = lax.axis_index("blk")
    at_x, at_z, at_core = me // (PAIR * CORES), me // CORES % PAIR, me % CORES

    def place(x, z, core):
        return index(at_x + x, at_z + z, at_core + core)

    def other(array):
        return fetch(array, core=1)

    order = [(2, 0, 1), (-1, 1, 1), (1, 1, 1), (2, 1, 0), (2, 1, 1)]
    order += [(0, 0, 0), (0, 0, 1)]
    order += [(2, 0, 0), (-1, 1, 0), (1, 1, 0)]
    order += [(1, 0, 0), (-1, 0, 0), (0, 1, 0), (1, 0, 1), (-1, 0, 1), (0, 1, 1)]
    places = jnp.stack([place(*o) for o in order]).astype(jnp.int32)
    after = lax.optimization_barrier
    near = [fetch(own, x=1), fetch(own, x=-1), fetch(own, z=1)]
    beside = other(own)
    xh, x8, a, v, k0 = opening(2, points, [own, beside])
    *near, v, places = after((*near, v, places))
    up, down, across = near
    far = [fetch(up, x=1), fetch(across, x=-1), fetch(up, z=1)]
    near_other = [other(b) for b in near]
    v, k1 = middle(4, xh, x8, a, v, near + near_other, False)
    *far, v = after((*far, v))
    last = [fetch(far[2][0:1], x=1), fetch(far[1][1:2], x=-1)]
    far_other = [other(b) for b in far]
    v, k2 = middle(3, xh, x8, a, v, far, True)
    *last, v = after((*last, v))
    last_other = [other(b) for b in last]
    sums = closing(10, 8, places, rows_size, xh, x8, a, v, far_other + last + last_other, [k0, k2], [k1])
    parts = lax.all_to_all(sums.reshape(-1, 1, 2 * UNIT), ("blk", "rows"), 0, 0, tiled=True)
    return jnp.sum(parts, axis=(0, 1)) / total_points


def solution(mesh):
    return jax.shard_map(
        body,
        mesh=mesh,
        in_specs=(P(("blk", "rows"), None), P("blk", None), P("blk")),
        out_specs=P("blk"),
        check_vma=False,
    )
```
